128 devices in a mesh: rcv: 8 (over z, core), src: 16 (over y, x).
Axes of the slice: x: 4, y: 4, z: 4, core: 2. Of those that a mesh axis runs over, the one named last changes fastest.
Arguments:
- response: float32 [8, 8192, 8192], P(None, 'rcv', 'src'), may hold values from -0.0234375 to 0.0234375
- focusing: float32 [16, 71, 8192], P(None, None, ('src', 'rcv')), may hold values from -6 to 6
Outputs:
- convolved: float32 [64, 16, 8192], P('src', None, 'rcv')
The draws below stay inside these ranges and needn't reach their ends.
All inputs are finite; a program needn't handle non-finite values.
Results may differ from the reference program's by a relative error of at most 0.00011.
Values sent between devices are 32-bit elements; how exact they have to be, the bound alone decides.
A program may use at most 64 MiB of HBM per device.

```python
import jax
import jax.numpy as jnp
from jax import lax

NR = 8192
NS = 8192
KT = 8
NT = 64
NF = 16
TIN = 71


def steps_of(rng, dims, shards, low, high):
    level, own = 1.0, jax.random.fold_in(rng, 6)
    for dim, parts in shards:
        heights = jnp.exp(jax.random.uniform(jax.random.fold_in(own, dim), (parts,), jnp.float32, low / len(shards), high / len(shards)))
        level = level * jnp.repeat(heights, dims[dim] // parts).reshape([-1 if axis == dim else 1 for axis in range(len(dims))])
    return level


def scatter_about(own_key, extent, deviation, most, pieces=(), dtype=jnp.bfloat16):
    entries = deviation * jax.random.normal(own_key, extent, jnp.float32)
    if pieces:
        entries = entries * steps_of(own_key, extent, pieces, -0.22, 0.18)
    return jnp.clip(entries, -most, most).astype(dtype)


def setup_inputs(seed: int = 0) -> dict:
    streams_of = jax.random.split(jax.random.key(seed), 3)
    response = scatter_about(streams_of[0], (KT, NR, NS), (NS * KT) ** -0.5, 0.0234375, ((1, 8), (2, 16)), jnp.float32)
    focusing = scatter_about(streams_of[1], (NF, TIN, NS), 1.0, 6.0, ((2, 128),), jnp.float32)
    return {"response": response, "focusing": focusing}


def reference(response, focusing):
    total = jnp.zeros((NF * NT, NR), jnp.float32)
    for k in range(KT):
        window = focusing[:, KT - 1 - k:KT - 1 - k + NT, :].reshape(NF * NT, NS)
        total = total + jnp.dot(window, response[k].T, preferred_element_type=jnp.float32, precision=lax.Precision.HIGHEST)
    return jnp.transpose(total.reshape(NF, NT, NR), (1, 0, 2))
```

```python
import jax
import jax.numpy as jnp
from jax import lax
from jax.experimental import pallas as pl
from jax.experimental.pallas import tpu as pltpu
from jax.sharding import PartitionSpec as P

MESH = pl.DeviceIdType.MESH
F32, BF16 = jnp.float32, jnp.bfloat16
OFFSETS = (0, 1, 3, 2)
NT = (((1,), (1,)), ((), ()))


def split(v):
    high = v.astype(BF16)
    return high, (v - high.astype(F32)).astype(BF16)


def kernel(resp, foc, out, raw, band, hist, flat, lags, part, got1, got2,
           raw_sem, z_send, pair_send, hist_recv, send1, recv1, send2, recv2):
    rcv, src = lax.axis_index("rcv"), lax.axis_index("src")
    z, core = rcv // 2, lax.rem(rcv, 2)
    y, x = src // 4, lax.rem(src, 4)

    def along_z(d):
        return {"rcv": lax.rem(z + d, 4) * 2 + core}

    def along_x(d):
        return {"src": y * 4 + lax.rem(x + d, 4)}

    def along_y(d):
        return {"src": lax.rem(y + d, 4) * 4 + x}

    pair = {"rcv": z * 2 + 1 - core}
    partners = [pair] + [f(d) for f in (along_z, along_x, along_y) for d in (1, 2, 3)]

    barrier = pltpu.get_barrier_semaphore()
    for device in partners:
        pl.semaphore_signal(barrier, inc=1, device_id=device, device_id_type=MESH)

    def fetch(place, slot):
        lanes = pl.multiple_of(lax.rem(z + OFFSETS[place], 4) * 128, 128)
        return pltpu.make_async_copy(resp.at[:, :, pl.ds(lanes, 128)], raw.at[slot], raw_sem.at[place])

    for place in range(2):
        fetch(place, place).start()

    def remote(src_ref, dst_ref, send, recv, device):
        return pltpu.make_async_remote_copy(
            src_ref=src_ref, dst_ref=dst_ref, send_sem=send, recv_sem=recv,
            device_id=device, device_id_type=MESH)

    for f in range(16):
        steps = foc[f].T
        both = jnp.concatenate([steps[0:36, :], steps[35:71, :]], axis=1)
        hist[f // 8, 0, 0, pl.ds(f % 8, 36, stride=8), :] = both

    def to_z(h, d):
        return remote(hist.at[h, 0, 0], hist.at[h, (4 - d) % 4, 0], z_send.at[h, d - 1],
                      hist_recv.at[h, (4 - d) % 4, 0], along_z(d))

    def to_pair(h, o):
        return remote(hist.at[h, o, 0], hist.at[h, o, 1], pair_send.at[h, o], hist_recv.at[h, o, 1], pair)

    pl.semaphore_wait(barrier, len(partners))
    for h in range(2):
        to_pair(h, 0).start()
        for d in (1, 3, 2):
            to_z(h, d).start()

    def split_band(place, slot, block, rows):
        for r in range(0, rows, 32):
            at = pl.ds(pl.multiple_of(block * rows + r, 32), 32)
            for j in range(4):
                first, second = raw[slot, j, at, :], raw[slot, 4 + j, at, :]
                lanes = pl.ds(place * 512 + j * 128, 128)
                for p, v in enumerate((first + second, second, first)):
                    high, low = split(v)
                    band[p, 0, at, lanes] = high
                    band[p, 1, at, lanes] = low

    def split_lags(h, place):
        o = OFFSETS[place]
        lane = lax.broadcasted_iota(jnp.int32, (288, 128), 1)
        a, b = hist[h, o, core], hist[h, o, 1 - core]
        flat[0:288, :] = jnp.where(lane < 64, a, pltpu.roll(b, 64, 1))
        flat[280:568, :] = jnp.where(lane < 64, pltpu.roll(a, 64, 1), b)
        for j in range(4):
            lanes = pl.ds(place * 512 + j * 128, 128)

            def window(m, _):
                at = pl.ds(pl.multiple_of(m * 32, 32), 32)

                def rows(t):
                    return flat[pl.ds(pl.multiple_of(m * 64 + t * 8, 8), 32), :]

                now = rows(7 - j)
                for p, v in enumerate((now, rows(3 - j) - now, now - rows(11 - j))):
                    high, low = split(v)
                    lags[h, p, 0, at, lanes] = high
                    lags[h, p, 1, at, lanes] = low
                return 0

            lax.fori_loop(0, 8, window, 0)

    def product(h, quarter, p, first, last):
        at = pl.ds(pl.multiple_of(quarter * 256, 256), 256)
        lanes = pl.ds(first * 512, (last - first) * 512)
        total = None
        for i, j in ((0, 0), (0, 1), (1, 0)):
            term = lax.dot_general(lags[h, p, i, :, lanes], band[p, j, at, lanes], NT, preferred_element_type=F32)
            total = term if total is None else total + term
        return total

    def add_products(h, quarter, first, last, fresh):
        chunk = h * 4 + quarter
        for p, odds in ((0, (0, 1)), (1, (0,)), (2, (1,))):
            total = product(h, quarter, p, first, last)
            for m in range(8):
                for b in odds:
                    to_x, to_y = 2 * (m % 2) + b, m // 2
                    block = total[m * 32:(m + 1) * 32, :]
                    for way, (one, two) in enumerate(((to_x, to_y), (to_y, to_x))):
                        v = block[:, way * 128:(way + 1) * 128]
                        if p == 2:
                            v = part[chunk, way, one, two] - v
                        elif p == 1 or not fresh:
                            v = part[chunk, way, one, two] + v
                        part[chunk, way, one, two] = v

    lanes_of = (x, y)
    ring1, ring2 = (along_x, along_y), (along_y, along_x)

    def stage1(chunk, way, d):
        return remote(part.at[chunk, way, lax.rem(lanes_of[way] + d, 4)], got1.at[chunk, way, d - 1],
                      send1.at[chunk, way, d - 1], recv1.at[chunk, way, d - 1], ring1[way](d))

    def stage2(chunk, way, d):
        return remote(part.at[chunk, way, lanes_of[way], lax.rem(lanes_of[1 - way] + d, 4)], got2.at[chunk, way, d - 1],
                      send2.at[chunk, way, d - 1], recv2.at[chunk, way, d - 1], ring2[way](d))

    def begin(chunk):
        for d in (2, 1, 3):
            for way in range(2):
                stage1(chunk, way, d).start()

    def turn(chunk):
        for way in range(2):
            for d in (1, 3, 2):
                stage1(chunk, way, d).wait_recv()
            part[chunk, way, lanes_of[way]] += got1[chunk, way, 0] + (got1[chunk, way, 1] + got1[chunk, way, 2])
            for d in (2, 1, 3):
                stage2(chunk, way, d).start()

    def finish(h, quarter):
        chunk = h * 4 + quarter
        for way in range(2):
            for d in (1, 3, 2):
                stage2(chunk, way, d).wait_recv()
            v = ((part[chunk, way, lanes_of[way], lanes_of[1 - way]] + got2[chunk, way, 0])
                 + (got2[chunk, way, 1] + got2[chunk, way, 2]))
            out[:, h * 8:(h + 1) * 8, quarter * 256 + way * 128:quarter * 256 + way * 128 + 128] = v.reshape(4, 8, 128)

    fetch(0, 0).wait()
    lax.fori_loop(0, 8, lambda i, _: (split_band(0, 0, i, 128), 0)[1], 0)
    fetch(2, 0).start()
    to_pair(0, 0).wait_recv()
    split_lags(0, 0)
    fetch(1, 1).wait()

    def own(h, first, place, rows):
        def step(i, _):
            add_products(h, first + i, 0, 1, True)
            split_band(place, (place % 2), i, rows)
            return 0
        return step

    lax.fori_loop(0, 4, own(0, 0, 1, 256), 0)
    fetch(3, 1).start()
    to_pair(1, 0).wait_recv()
    split_lags(1, 0)
    fetch(2, 0).wait()
    lax.fori_loop(0, 2, own(1, 0, 2, 512), 0)
    fetch(3, 1).wait()
    lax.fori_loop(0, 2, own(1, 2, 3, 512), 0)

    def pass_on(h):
        for d in (1, 3, 2):
            to_z(h, d).wait_recv()
        for place in (1, 2, 3):
            to_pair(h, OFFSETS[place]).start()
        for place in (1, 2, 3):
            to_pair(h, OFFSETS[place]).wait_recv()
            split_lags(h, place)

    def rest(h):
        def step(i, _):
            chunk = h * 4 + i
            add_products(h, i, 1, 4, False)
            begin(chunk)

            @pl.when(chunk >= 2)
            def _():
                turn(chunk - 2)
            return 0

        lax.fori_loop(0, 4, step, 0)

    pass_on(0)
    rest(0)
    pass_on(1)
    rest(1)
    turn(6)
    turn(7)
    for h in range(2):
        for quarter in range(4):
            finish(h, quarter)

    for h in range(2):
        for d in (1, 2, 3):
            to_z(h, d).wait_send()
        for o in range(4):
            to_pair(h, o).wait_send()

    def drain(chunk, _):
        for way in range(2):
            for d in (1, 2, 3):
                stage1(chunk, way, d).wait_send()
                stage2(chunk, way, d).wait_send()
        return 0

    lax.fori_loop(0, 8, drain, 0)


def on_device(response, focusing):
    dma = pltpu.SemaphoreType.DMA
    return pl.pallas_call(
        kernel,
        out_shape=jax.ShapeDtypeStruct((4, 16, 1024), F32),
        in_specs=[pl.BlockSpec(memory_space=pl.ANY), pl.BlockSpec(memory_space=pltpu.VMEM)],
        out_specs=pl.BlockSpec(memory_space=pltpu.VMEM),
        scratch_shapes=[
            pltpu.VMEM((2, 8, 1024, 128), F32),
            pltpu.VMEM((3, 2, 1024, 2048), BF16),
            pltpu.VMEM((2, 4, 2, 288, 128), F32),
            pltpu.VMEM((568, 128), F32),
            pltpu.VMEM((2, 3, 2, 256, 2048), BF16),
            pltpu.VMEM((8, 2, 4, 4, 32, 128), F32),
            pltpu.VMEM((8, 2, 3, 4, 32, 128), F32),
            pltpu.VMEM((8, 2, 3, 32, 128), F32),
            dma((4,)), dma((2, 3)), dma((2, 4)), dma((2, 4, 2)),
            dma((8, 2, 3)), dma((8, 2, 3)), dma((8, 2, 3)), dma((8, 2, 3)),
        ],
        compiler_params=pltpu.CompilerParams(
            collective_id=0, has_side_effects=True, vmem_limit_bytes=63 * 2**20),
    )(response, jnp.swapaxes(focusing, 1, 2))


def solution(mesh):
    in_specs = (P(None, "rcv", "src"), P(None, None, ("src", "rcv")))
    return jax.shard_map(
        on_device, mesh=mesh, in_specs=in_specs, out_specs=P("src", None, "rcv"), check_vma=False
    )
```

```python
import jax
import jax.numpy as jnp
from jax import lax
from jax.experimental import pallas as pl
from jax.experimental.pallas import tpu as pltpu
from jax.sharding import PartitionSpec as P

MESH = pl.DeviceIdType.MESH
F32, BF16 = jnp.float32, jnp.bfloat16
OFFSETS = (0, 1, 3, 2)
NT = (((1,), (1,)), ((), ()))


def split(v):
    high = v.astype(BF16)
    return high, (v - high.astype(F32)).astype(BF16)


def kernel(resp, foc, out, raw, band, hist, flat, lags, part, got1, got2,
           raw_sem, z_send, pair_send, hist_recv, send1, recv1, send2, recv2):
    rcv, src = lax.axis_index("rcv"), lax.axis_index("src")
    z, core = rcv // 2, lax.rem(rcv, 2)
    y, x = src // 4, lax.rem(src, 4)

    xs, ys, zs = ([lax.rem(v + d, 4) for d in range(4)] for v in (x, y, z))
    on_x = [{"src": y * 4 + v, "rcv": rcv} for v in xs]
    on_y = [{"src": v * 4 + x, "rcv": rcv} for v in ys]
    on_z = [{"src": src, "rcv": v * 2 + core} for v in zs]
    pair = {"src": src, "rcv": z * 2 + 1 - core}
    partners = [pair] + on_z[1:] + on_x[1:] + on_y[1:]

    barrier = pltpu.get_barrier_semaphore()
    for device in partners:
        pl.semaphore_signal(barrier, inc=1, device_id=device, device_id_type=MESH)

    def fetch(place, slot):
        lanes = pl.multiple_of(zs[OFFSETS[place]] * 128, 128)
        return pltpu.make_async_copy(resp.at[:, :, pl.ds(lanes, 128)], raw.at[slot], raw_sem.at[place])

    for place in range(2):
        fetch(place, place).start()

    def remote(src_ref, dst_ref, send, recv, device):
        return pltpu.make_async_remote_copy(
            src_ref=src_ref, dst_ref=dst_ref, send_sem=send, recv_sem=recv,
            device_id=device, device_id_type=MESH)

    for f in range(16):
        steps = foc[f].T
        both = jnp.concatenate([steps[0:36, :], steps[35:71, :]], axis=1)
        hist[f // 8, 0, 0, pl.ds(f % 8, 36, stride=8), :] = both

    def to_z(h, d):
        return remote(hist.at[h, 0, 0], hist.at[h, (4 - d) % 4, 0], z_send.at[h, d - 1],
                      hist_recv.at[h, (4 - d) % 4, 0], on_z[d])

    def to_pair(h, o):
        return remote(hist.at[h, o, 0], hist.at[h, o, 1], pair_send.at[h, o], hist_recv.at[h, o, 1], pair)

    def split_band(place, slot):
        def step(i, _):
            for r in range(8):
                at = pl.ds(pl.multiple_of(i * 128 + r * 16, 16), 16)
                for j in range(4):
                    first, second = raw[slot, j, at, :], raw[slot, 4 + j, at, :]
                    lanes = pl.ds(place * 512 + j * 128, 128)
                    for p, v in enumerate((first + second, second, first)):
                        high, low = split(v)
                        band[p, 0, at, lanes] = high
                        band[p, 1, at, lanes] = low
            return 0

        lax.fori_loop(0, 8, step, 0)

    def split_lags(h, place):
        o = OFFSETS[place]
        lane = lax.broadcasted_iota(jnp.int32, (288, 128), 1)
        a, b = hist[h, o, core], hist[h, o, 1 - core]
        flat[0:288, :] = jnp.where(lane < 64, a, pltpu.roll(b, 64, 1))
        flat[280:568, :] = jnp.where(lane < 64, pltpu.roll(a, 64, 1), b)

        def window(m, _):
            at = pl.ds(pl.multiple_of(m * 32, 32), 32)

            def rows(t):
                return flat[pl.ds(pl.multiple_of(m * 64 + t * 8, 8), 32), :]

            for j in range(4):
                lanes = pl.ds(place * 512 + j * 128, 128)
                now = rows(7 - j)
                for p, v in enumerate((now, rows(3 - j) - now, now - rows(11 - j))):
                    high, low = split(v)
                    lags[h, p, 0, at, lanes] = high
                    lags[h, p, 1, at, lanes] = low
            return 0

        lax.fori_loop(0, 8, window, 0)

    def product(h, quarter, p, first, last):
        at = pl.ds(pl.multiple_of(quarter * 256, 256), 256)
        lanes = pl.ds(first * 512, (last - first) * 512)
        total = None
        for i, j in ((0, 0), (0, 1), (1, 0)):
            term = lax.dot_general(lags[h, p, i, :, lanes], band[p, j, at, lanes], NT, preferred_element_type=F32)
            total = term if total is None else total + term
        return total

    def add_products(h, quarter, first, last, fresh=False, between=None):
        chunk = h * 4 + quarter
        for p, odds in ((0, (0, 1)), (1, (0,)), (2, (1,))):
            total = product(h, quarter, p, first, last)
            for m in range(8):
                for b in odds:
                    to_x, to_y = 2 * (m % 2) + b, m // 2
                    block = total[m * 32:(m + 1) * 32, :]
                    for way, (one, two) in enumerate(((to_x, to_y), (to_y, to_x))):
                        v = block[:, way * 128:(way + 1) * 128]
                        if p == 2:
                            v = part[chunk, way, one, two] - v
                        elif p == 1 or not fresh:
                            v = part[chunk, way, one, two] + v
                        part[chunk, way, one, two] = v
            if between is not None:
                between(p)

    ring, at_ring = (on_x, on_y), (xs, ys)

    def stage1(chunk, way, d):
        return remote(part.at[chunk, way, at_ring[way][d]], got1.at[chunk, way, d - 1],
                      send1.at[chunk, way, d - 1, 0], recv1.at[chunk, way, d - 1, 0], ring[way][d])

    def relay(chunk, way, kind, turn):
        d = 3 if turn else 1
        half = 1 - turn if kind == 1 else turn
        owner = at_ring[way][2 if kind == 0 else d]
        return remote(part.at[chunk, way, owner, pl.ds(2 * half, 2)], got1.at[chunk, way, kind, pl.ds(2 * half, 2)],
                      send1.at[chunk, way, kind, turn], recv1.at[chunk, way, kind, turn], ring[way][d])

    def stage2(chunk, way, d):
        return remote(part.at[chunk, way, at_ring[way][0], at_ring[1 - way][d]], got2.at[chunk, way, d - 1],
                      send2.at[chunk, way, d - 1], recv2.at[chunk, way, d - 1], ring[1 - way][d])

    both = [(way, turn) for way in range(2) for turn in range(2)]

    def begin(chunk):
        for kind in (0, 1):
            for way, turn in both:
                relay(chunk, way, kind, turn).start()

    def pass_sums(chunk):
        for way, turn in both:
            relay(chunk, way, 0, turn).wait_recv()
        for way, turn in both:
            owner = at_ring[way][3 if turn else 1]
            part[chunk, way, owner, 2 * turn:2 * turn + 2] += got1[chunk, way, 0, 2 * turn:2 * turn + 2]
        for way, turn in both:
            relay(chunk, way, 2, turn).start()

    def begin_direct(chunk):
        for d in (2, 1, 3):
            for way in range(2):
                stage1(chunk, way, d).start()

    def second(chunk):
        for d in (2, 1, 3):
            for way in range(2):
                stage2(chunk, way, d).start()

    def cross(chunk):
        for way, turn in both:
            relay(chunk, way, 1, turn).wait_recv()
            relay(chunk, way, 2, turn).wait_recv()
        for way in range(2):
            part[chunk, way, at_ring[way][0]] += got1[chunk, way, 1] + got1[chunk, way, 2]
        second(chunk)

    def cross_direct(chunk):
        for way in range(2):
            for d in (1, 3, 2):
                stage1(chunk, way, d).wait_recv()
        for way in range(2):
            part[chunk, way, at_ring[way][0]] += got1[chunk, way, 0] + (got1[chunk, way, 1] + got1[chunk, way, 2])
        second(chunk)

    def finish(h, quarter):
        chunk = h * 4 + quarter
        for way in range(2):
            for d in (1, 3, 2):
                stage2(chunk, way, d).wait_recv()
            v = ((part[chunk, way, at_ring[way][0], at_ring[1 - way][0]] + got2[chunk, way, 0])
                 + (got2[chunk, way, 1] + got2[chunk, way, 2]))
            out[:, h * 8:(h + 1) * 8, quarter * 256 + way * 128:quarter * 256 + way * 128 + 128] = v.reshape(4, 8, 128)

    def gather(h):
        for d in (1, 3, 2):
            to_z(h, d).start()

    def pass_on(h, places):
        for place in places:
            o = OFFSETS[place]
            to_z(h, 4 - o).wait_recv()
            to_pair(h, o).start()

    def arrive(h, places):
        for place in places:
            to_pair(h, OFFSETS[place]).wait_recv()
            split_lags(h, place)

    fetch(0, 0).wait()
    split_band(0, 0)
    fetch(2, 0).start()
    fetch(1, 1).wait()
    split_band(1, 1)
    fetch(3, 1).start()
    fetch(2, 0).wait()
    split_band(2, 0)
    pl.semaphore_wait(barrier, len(partners))
    gather(0)
    for h in range(2):
        to_pair(h, 0).start()
    fetch(3, 1).wait()
    split_band(3, 1)

    def own(h, first, count):
        def step(i, _):
            for n in range(count):
                add_products(h, first + i * count + n, 0, 1, fresh=True)
            return 0

        return step

    arrive(0, (0,))
    lax.fori_loop(0, 2, own(0, 0, 2), 0)
    gather(1)
    arrive(1, (0,))
    lax.fori_loop(0, 1, own(1, 0, 2), 0)
    pass_on(0, (1, 2))
    lax.fori_loop(0, 1, own(1, 2, 2), 0)
    arrive(0, (1, 2))
    add_products(0, 0, 1, 3)
    pass_on(0, (3,))
    add_products(0, 1, 1, 3)
    arrive(0, (3,))
    for quarter in range(2):
        add_products(0, quarter, 3, 4)
        begin(quarter)

    def rest(chunk, _):
        @pl.when(chunk == 3)
        def _():
            pass_on(1, (1, 2, 3))

        @pl.when(chunk == 4)
        def _():
            arrive(1, (1, 2, 3))

        add_products(chunk // 4, lax.rem(chunk, 4), 1, 4)

        @pl.when(chunk < 7)
        def _():
            begin(chunk)

        pass_sums(chunk - 2)

        @pl.when(chunk >= 4)
        def _():
            cross(chunk - 4)
        return 0

    lax.fori_loop(2, 8, rest, 0)
    begin_direct(7)
    cross(4)
    pass_sums(6)
    cross(5)
    cross_direct(7)
    cross(6)
    for h in range(2):
        for quarter in range(4):
            finish(h, quarter)

    for h in range(2):
        for d in (1, 2, 3):
            to_z(h, d).wait_send()
        for o in range(4):
            to_pair(h, o).wait_send()

    def sent(chunk, _):
        for way, turn in both:
            for kind in range(3):
                relay(chunk, way, kind, turn).wait_send()
        return 0

    lax.fori_loop(0, 7, sent, 0)
    for way in range(2):
        for d in (1, 2, 3):
            stage1(7, way, d).wait_send()

    def sent_second(chunk, _):
        for way in range(2):
            for d in (1, 2, 3):
                stage2(chunk, way, d).wait_send()
        return 0

    lax.fori_loop(0, 8, sent_second, 0)


def on_device(response, focusing):
    dma = pltpu.SemaphoreType.DMA
    return pl.pallas_call(
        kernel,
        out_shape=jax.ShapeDtypeStruct((4, 16, 1024), F32),
        in_specs=[pl.BlockSpec(memory_space=pl.ANY), pl.BlockSpec(memory_space=pltpu.VMEM)],
        out_specs=pl.BlockSpec(memory_space=pltpu.VMEM),
        scratch_shapes=[
            pltpu.VMEM((2, 8, 1024, 128), F32),
            pltpu.VMEM((3, 2, 1024, 2048), BF16),
            pltpu.VMEM((2, 4, 2, 288, 128), F32),
            pltpu.VMEM((568, 128), F32),
            pltpu.VMEM((2, 3, 2, 256, 2048), BF16),
            pltpu.VMEM((8, 2, 4, 4, 32, 128), F32),
            pltpu.VMEM((8, 2, 3, 4, 32, 128), F32),
            pltpu.VMEM((8, 2, 3, 32, 128), F32),
            dma((4,)), dma((2, 3)), dma((2, 4)), dma((2, 4, 2)),
            dma((8, 2, 3, 2)), dma((8, 2, 3, 2)), dma((8, 2, 3)), dma((8, 2, 3)),
        ],
        compiler_params=pltpu.CompilerParams(
            collective_id=0, has_side_effects=True, vmem_limit_bytes=63 * 2**20),
    )(response, jnp.swapaxes(focusing, 1, 2))


def solution(mesh):
    in_specs = (P(None, "rcv", "src"), P(None, None, ("src", "rcv")))
    return jax.shard_map(
        on_device, mesh=mesh, in_specs=in_specs, out_specs=P("src", None, "rcv"), check_vma=False
    )
```

```python
import jax
import jax.numpy as jnp
from jax import lax
from jax.experimental import pallas as pl
from jax.experimental.pallas import tpu as pltpu
from jax.sharding import PartitionSpec as P

MESH = pl.DeviceIdType.MESH
F32, BF16 = jnp.float32, jnp.bfloat16
OFFSETS = (0, 1, 3, 2)
NT = (((1,), (1,)), ((), ()))


def split(v):
    high = v.astype(BF16)
    return high, (v - high.astype(F32)).astype(BF16)


def kernel(resp, foc, out, raw, band, hist, flat, lags, part, got1, got2,
           raw_sem, z_send, pair_send, hist_recv, send1, recv1, send2, recv2):
    rcv, src = lax.axis_index("rcv"), lax.axis_index("src")
    z, core = rcv // 2, lax.rem(rcv, 2)
    y, x = src // 4, lax.rem(src, 4)

    xs, ys, zs = ([lax.rem(v + d, 4) for d in range(4)] for v in (x, y, z))
    on_x = [{"src": y * 4 + v, "rcv": rcv} for v in xs]
    on_y = [{"src": v * 4 + x, "rcv": rcv} for v in ys]
    on_z = [{"src": src, "rcv": v * 2 + core} for v in zs]
    pair = {"src": src, "rcv": z * 2 + 1 - core}
    partners = [pair] + on_z[1:] + on_x[1:] + on_y[1:]

    barrier = pltpu.get_barrier_semaphore()
    for device in partners:
        pl.semaphore_signal(barrier, inc=1, device_id=device, device_id_type=MESH)

    def fetch(place, slot):
        lanes = pl.multiple_of(zs[OFFSETS[place]] * 128, 128)
        return pltpu.make_async_copy(resp.at[:, :, pl.ds(lanes, 128)], raw.at[slot], raw_sem.at[place])

    for place in range(2):
        fetch(place, place).start()

    def remote(src_ref, dst_ref, send, recv, device):
        return pltpu.make_async_remote_copy(
            src_ref=src_ref, dst_ref=dst_ref, send_sem=send, recv_sem=recv,
            device_id=device, device_id_type=MESH)

    for f in range(16):
        steps = foc[f].T
        both = jnp.concatenate([steps[0:36, :], steps[35:71, :]], axis=1)
        hist[f // 8, 0, 0, pl.ds(f % 8, 36, stride=8), :] = both

    def to_z(h, d):
        return remote(hist.at[h, 0, 0], hist.at[h, (4 - d) % 4, 0], z_send.at[h, d - 1],
                      hist_recv.at[h, (4 - d) % 4, 0], on_z[d])

    def to_pair(h, o):
        return remote(hist.at[h, o, 0], hist.at[h, o, 1], pair_send.at[h, o], hist_recv.at[h, o, 1], pair)

    def split_band(place, slot):
        def step(i, _):
            for r in range(8):
                at = pl.ds(pl.multiple_of(i * 128 + r * 16, 16), 16)
                for j in range(4):
                    first, second = raw[slot, j, at, :], raw[slot, 4 + j, at, :]
                    lanes = pl.ds(place * 512 + j * 128, 128)
                    for p, v in enumerate((first + second, second, first)):
                        high, low = split(v)
                        band[p, 0, at, lanes] = high
                        band[p, 1, at, lanes] = low
            return 0

        lax.fori_loop(0, 8, step, 0)

    def split_lags(h, place):
        o = OFFSETS[place]
        lane = lax.broadcasted_iota(jnp.int32, (288, 128), 1)
        a, b = hist[h, o, core], hist[h, o, 1 - core]
        flat[0:288, :] = jnp.where(lane < 64, a, pltpu.roll(b, 64, 1))
        flat[280:568, :] = jnp.where(lane < 64, pltpu.roll(a, 64, 1), b)

        def window(m, _):
            at = pl.ds(pl.multiple_of(m * 32, 32), 32)

            def rows(t):
                return flat[pl.ds(pl.multiple_of(m * 64 + t * 8, 8), 32), :]

            for j in range(4):
                lanes = pl.ds(place * 512 + j * 128, 128)
                now = rows(7 - j)
                for p, v in enumerate((now, rows(3 - j) - now, now - rows(11 - j))):
                    high, low = split(v)
                    lags[h, p, 0, at, lanes] = high
                    lags[h, p, 1, at, lanes] = low
            return 0

        lax.fori_loop(0, 8, window, 0)

    def product(h, quarter, p, first, last):
        at = pl.ds(pl.multiple_of(quarter * 256, 256), 256)
        lanes = pl.ds(first * 512, (last - first) * 512)
        total = None
        for i, j in ((0, 0), (0, 1), (1, 0)):
            term = lax.dot_general(lags[h, p, i, :, lanes], band[p, j, at, lanes], NT, preferred_element_type=F32)
            total = term if total is None else total + term
        return total

    def add_products(h, quarter, first, last, fresh=False, between=None):
        chunk = h * 4 + quarter
        for p, odds in ((0, (0, 1)), (1, (0,)), (2, (1,))):
            total = product(h, quarter, p, first, last)
            for m in range(8):
                for b in odds:
                    to_x, to_y = 2 * (m % 2) + b, m // 2
                    block = total[m * 32:(m + 1) * 32, :]
                    for way, (one, two) in enumerate(((to_x, to_y), (to_y, to_x))):
                        v = block[:, way * 128:(way + 1) * 128]
                        if p == 2:
                            v = part[chunk, way, one, two] - v
                        elif p == 1 or not fresh:
                            v = part[chunk, way, one, two] + v
                        part[chunk, way, one, two] = v
            if between is not None:
                between(p)

    ring, at_ring = (on_x, on_y), (xs, ys)

    def stage1(chunk, way, d):
        return remote(part.at[chunk, way, at_ring[way][d]], got1.at[chunk, way, d - 1],
                      send1.at[chunk, way, d - 1, 0], recv1.at[chunk, way, d - 1, 0], ring[way][d])

    def relay(chunk, way, kind, turn):
        d = 3 if turn else 1
        half = 1 - turn if kind == 1 else turn
        owner = at_ring[way][2 if kind == 0 else d]
        return remote(part.at[chunk, way, owner, pl.ds(2 * half, 2)], got1.at[chunk, way, kind, pl.ds(2 * half, 2)],
                      send1.at[chunk, way, kind, turn], recv1.at[chunk, way, kind, turn], ring[way][d])

    def stage2(chunk, way, d):
        return remote(part.at[chunk, way, at_ring[way][0], at_ring[1 - way][d]], got2.at[chunk, way, d - 1],
                      send2.at[chunk, way, d - 1], recv2.at[chunk, way, d - 1], ring[1 - way][d])

    both = [(way, turn) for way in range(2) for turn in range(2)]

    def begin(chunk):
        for kind in (0, 1):
            for way, turn in both:
                relay(chunk, way, kind, turn).start()

    def pass_sums(chunk):
        for way, turn in both:
            relay(chunk, way, 0, turn).wait_recv()
        for way, turn in both:
            owner = at_ring[way][3 if turn else 1]
            part[chunk, way, owner, 2 * turn:2 * turn + 2] += got1[chunk, way, 0, 2 * turn:2 * turn + 2]
        for way, turn in both:
            relay(chunk, way, 2, turn).start()

    def begin_direct(chunk):
        for d in (2, 1, 3):
            for way in range(2):
                stage1(chunk, way, d).start()

    def second(chunk):
        for d in (2, 1, 3):
            for way in range(2):
                stage2(chunk, way, d).start()

    def cross(chunk):
        for way, turn in both:
            relay(chunk, way, 1, turn).wait_recv()
            relay(chunk, way, 2, turn).wait_recv()
        for way in range(2):
            part[chunk, way, at_ring[way][0]] += got1[chunk, way, 1] + got1[chunk, way, 2]
        second(chunk)

    def cross_direct(chunk):
        for way in range(2):
            for d in (1, 3, 2):
                stage1(chunk, way, d).wait_recv()
        for way in range(2):
            part[chunk, way, at_ring[way][0]] += got1[chunk, way, 0] + (got1[chunk, way, 1] + got1[chunk, way, 2])
        second(chunk)

    def finish(h, quarter):
        chunk = h * 4 + quarter
        for way in range(2):
            for d in (1, 3, 2):
                stage2(chunk, way, d).wait_recv()
            v = ((part[chunk, way, at_ring[way][0], at_ring[1 - way][0]] + got2[chunk, way, 0])
                 + (got2[chunk, way, 1] + got2[chunk, way, 2]))
            out[:, h * 8:(h + 1) * 8, quarter * 256 + way * 128:quarter * 256 + way * 128 + 128] = v.reshape(4, 8, 128)

    def gather(h):
        for d in (1, 3, 2):
            to_z(h, d).start()

    def pass_on(h, places):
        for place in places:
            o = OFFSETS[place]
            to_z(h, 4 - o).wait_recv()
            to_pair(h, o).start()

    def arrive(h, places):
        for place in places:
            to_pair(h, OFFSETS[place]).wait_recv()
            split_lags(h, place)

    pl.semaphore_wait(barrier, len(partners))
    gather(0)
    for h in range(2):
        to_pair(h, 0).start()
    fetch(0, 0).wait()
    split_band(0, 0)
    fetch(2, 0).start()
    fetch(1, 1).wait()
    split_band(1, 1)
    fetch(3, 1).start()

    def own(h, first, count):
        def step(i, _):
            for n in range(count):
                add_products(h, first + i * count + n, 0, 1, fresh=True)
            return 0

        return step

    arrive(0, (0,))
    lax.fori_loop(0, 2, own(0, 0, 2), 0)
    pass_on(0, (1, 2))
    gather(1)
    fetch(2, 0).wait()
    split_band(2, 0)
    arrive(1, (0,))
    lax.fori_loop(0, 2, own(1, 0, 2), 0)
    pass_on(0, (3,))
    fetch(3, 1).wait()
    split_band(3, 1)
    arrive(0, (1, 2, 3))
    for quarter in range(2):
        add_products(0, quarter, 1, 4)
        begin(quarter)

    def rest(chunk, _):
        @pl.when(chunk == 3)
        def _():
            pass_on(1, (1, 2, 3))

        @pl.when(chunk == 4)
        def _():
            arrive(1, (1, 2, 3))

        add_products(chunk // 4, lax.rem(chunk, 4), 1, 4)

        @pl.when(chunk < 7)
        def _():
            begin(chunk)

        pass_sums(chunk - 2)

        @pl.when(chunk >= 4)
        def _():
            cross(chunk - 4)
        return 0

    lax.fori_loop(2, 8, rest, 0)
    begin_direct(7)
    cross(4)
    pass_sums(6)
    cross(5)
    cross_direct(7)
    cross(6)
    for h in range(2):
        for quarter in range(4):
            finish(h, quarter)

    for h in range(2):
        for d in (1, 2, 3):
            to_z(h, d).wait_send()
        for o in range(4):
            to_pair(h, o).wait_send()

    def sent(chunk, _):
        for way, turn in both:
            for kind in range(3):
                relay(chunk, way, kind, turn).wait_send()
        return 0

    lax.fori_loop(0, 7, sent, 0)
    for way in range(2):
        for d in (1, 2, 3):
            stage1(7, way, d).wait_send()

    def sent_second(chunk, _):
        for way in range(2):
            for d in (1, 2, 3):
                stage2(chunk, way, d).wait_send()
        return 0

    lax.fori_loop(0, 8, sent_second, 0)


def on_device(response, focusing):
    dma = pltpu.SemaphoreType.DMA
    return pl.pallas_call(
        kernel,
        out_shape=jax.ShapeDtypeStruct((4, 16, 1024), F32),
        in_specs=[pl.BlockSpec(memory_space=pl.ANY), pl.BlockSpec(memory_space=pltpu.VMEM)],
        out_specs=pl.BlockSpec(memory_space=pltpu.VMEM),
        scratch_shapes=[
            pltpu.VMEM((2, 8, 1024, 128), F32),
            pltpu.VMEM((3, 2, 1024, 2048), BF16),
            pltpu.VMEM((2, 4, 2, 288, 128), F32),
            pltpu.VMEM((568, 128), F32),
            pltpu.VMEM((2, 3, 2, 256, 2048), BF16),
            pltpu.VMEM((8, 2, 4, 4, 32, 128), F32),
            pltpu.VMEM((8, 2, 3, 4, 32, 128), F32),
            pltpu.VMEM((8, 2, 3, 32, 128), F32),
            dma((4,)), dma((2, 3)), dma((2, 4)), dma((2, 4, 2)),
            dma((8, 2, 3, 2)), dma((8, 2, 3, 2)), dma((8, 2, 3)), dma((8, 2, 3)),
        ],
        compiler_params=pltpu.CompilerParams(
            collective_id=0, has_side_effects=True, vmem_limit_bytes=63 * 2**20),
    )(response, jnp.swapaxes(focusing, 1, 2))


def solution(mesh):
    in_specs = (P(None, "rcv", "src"), P(None, None, ("src", "rcv")))
    return jax.shard_map(
        on_device, mesh=mesh, in_specs=in_specs, out_specs=P("src", None, "rcv"), check_vma=False
    )
```

```python
import jax
import jax.numpy as jnp
from jax import lax
from jax.experimental import pallas as pl
from jax.experimental.pallas import tpu as pltpu
from jax.sharding import PartitionSpec as P

MESH = pl.DeviceIdType.MESH
F32, BF16 = jnp.float32, jnp.bfloat16
OFFSETS = (0, 1, 3, 2)
NT = (((1,), (1,)), ((), ()))


def split(v):
    high = v.astype(BF16)
    return high, (v - high.astype(F32)).astype(BF16)


def kernel(resp, foc, out, raw, band, hist, flat, lags, part, got1, got2,
           raw_sem, z_send, pair_send, hist_recv, send1, recv1, send2, recv2):
    rcv, src = lax.axis_index("rcv"), lax.axis_index("src")
    z, core = rcv // 2, lax.rem(rcv, 2)
    y, x = src // 4, lax.rem(src, 4)

    xs, ys, zs = ([lax.rem(v + d, 4) for d in range(4)] for v in (x, y, z))
    on_x = [{"src": y * 4 + v, "rcv": rcv} for v in xs]
    on_y = [{"src": v * 4 + x, "rcv": rcv} for v in ys]
    on_z = [{"src": src, "rcv": v * 2 + core} for v in zs]
    pair = {"src": src, "rcv": z * 2 + 1 - core}
    partners = [pair] + on_z[1:] + on_x[1:] + on_y[1:]

    barrier = pltpu.get_barrier_semaphore()
    for device in partners:
        pl.semaphore_signal(barrier, inc=1, device_id=device, device_id_type=MESH)

    def fetch(place, slot):
        lanes = pl.multiple_of(zs[OFFSETS[place]] * 128, 128)
        return pltpu.make_async_copy(resp.at[:, :, pl.ds(lanes, 128)], raw.at[slot], raw_sem.at[place])

    for place in range(2):
        fetch(place, place).start()

    def remote(src_ref, dst_ref, send, recv, device):
        return pltpu.make_async_remote_copy(
            src_ref=src_ref, dst_ref=dst_ref, send_sem=send, recv_sem=recv,
            device_id=device, device_id_type=MESH)

    for f in range(16):
        steps = foc[f].T
        both = jnp.concatenate([steps[0:36, :], steps[35:71, :]], axis=1)
        hist[f // 8, 0, 0, pl.ds(f % 8, 36, stride=8), :] = both

    def to_z(h, d):
        return remote(hist.at[h, 0, 0], hist.at[h, (4 - d) % 4, 0], z_send.at[h, d - 1],
                      hist_recv.at[h, (4 - d) % 4, 0], on_z[d])

    def to_pair(h, o):
        return remote(hist.at[h, o, 0], hist.at[h, o, 1], pair_send.at[h, o], hist_recv.at[h, o, 1], pair)

    def split_band(place, slot):
        def step(i, _):
            for r in range(8):
                at = pl.ds(pl.multiple_of(i * 128 + r * 16, 16), 16)
                for j in range(4):
                    first, second = raw[slot, j, at, :], raw[slot, 4 + j, at, :]
                    lanes = pl.ds(place * 512 + j * 128, 128)
                    for p, v in enumerate((first + second, second, first)):
                        high, low = split(v)
                        band[p, 0, at, lanes] = high
                        band[p, 1, at, lanes] = low
            return 0

        lax.fori_loop(0, 8, step, 0)

    def split_lags(h, place):
        o = OFFSETS[place]
        lane = lax.broadcasted_iota(jnp.int32, (288, 128), 1)
        a, b = hist[h, o, core], hist[h, o, 1 - core]
        flat[0:288, :] = jnp.where(lane < 64, a, pltpu.roll(b, 64, 1))
        flat[280:568, :] = jnp.where(lane < 64, pltpu.roll(a, 64, 1), b)

        def window(m, _):
            at = pl.ds(pl.multiple_of(m * 32, 32), 32)

            def rows(t):
                return flat[pl.ds(pl.multiple_of(m * 64 + t * 8, 8), 32), :]

            for j in range(4):
                lanes = pl.ds(place * 512 + j * 128, 128)
                now = rows(7 - j)
                for p, v in enumerate((now, rows(3 - j) - now, now - rows(11 - j))):
                    high, low = split(v)
                    lags[h, p, 0, at, lanes] = high
                    lags[h, p, 1, at, lanes] = low
            return 0

        lax.fori_loop(0, 8, window, 0)

    def product(h, quarter, p, first, last):
        at = pl.ds(pl.multiple_of(quarter * 256, 256), 256)
        lanes = pl.ds(first * 512, (last - first) * 512)
        total = None
        for i, j in ((0, 0), (0, 1), (1, 0)):
            term = lax.dot_general(lags[h, p, i, :, lanes], band[p, j, at, lanes], NT, preferred_element_type=F32)
            total = term if total is None else total + term
        return total

    def add_products(h, quarter, first, last, fresh=False, between=None):
        chunk = h * 4 + quarter
        for p, odds in ((0, (0, 1)), (1, (0,)), (2, (1,))):
            total = product(h, quarter, p, first, last)
            for m in range(8):
                for b in odds:
                    to_x, to_y = 2 * (m % 2) + b, m // 2
                    block = total[m * 32:(m + 1) * 32, :]
                    for way, (one, two) in enumerate(((to_x, to_y), (to_y, to_x))):
                        v = block[:, way * 128:(way + 1) * 128]
                        if p == 2:
                            v = part[chunk, way, one, two] - v
                        elif p == 1 or not fresh:
                            v = part[chunk, way, one, two] + v
                        part[chunk, way, one, two] = v
            if between is not None:
                between(p)

    ring, at_ring = (on_x, on_y), (xs, ys)

    def stage1(chunk, way, d):
        return remote(part.at[chunk, way, at_ring[way][d]], got1.at[chunk, way, d - 1],
                      send1.at[chunk, way, d - 1, 0], recv1.at[chunk, way, d - 1, 0], ring[way][d])

    def relay(chunk, way, kind, turn):
        d = 3 if turn else 1
        half = 1 - turn if kind == 1 else turn
        owner = at_ring[way][2 if kind == 0 else d]
        return remote(part.at[chunk, way, owner, pl.ds(2 * half, 2)], got1.at[chunk, way, kind, pl.ds(2 * half, 2)],
                      send1.at[chunk, way, kind, turn], recv1.at[chunk, way, kind, turn], ring[way][d])

    def stage2(chunk, way, d):
        return remote(part.at[chunk, way, at_ring[way][0], at_ring[1 - way][d]], got2.at[chunk, way, d - 1],
                      send2.at[chunk, way, d - 1], recv2.at[chunk, way, d - 1], ring[1 - way][d])

    both = [(way, turn) for way in range(2) for turn in range(2)]

    def begin(chunk):
        for kind in (0, 1):
            for way, turn in both:
                relay(chunk, way, kind, turn).start()

    def pass_sums(chunk):
        for way, turn in both:
            relay(chunk, way, 0, turn).wait_recv()
        for way, turn in both:
            owner = at_ring[way][3 if turn else 1]
            part[chunk, way, owner, 2 * turn:2 * turn + 2] += got1[chunk, way, 0, 2 * turn:2 * turn + 2]
        for way, turn in both:
            relay(chunk, way, 2, turn).start()

    def begin_direct(chunk):
        for d in (2, 1, 3):
            for way in range(2):
                stage1(chunk, way, d).start()

    def second(chunk):
        for d in (2, 1, 3):
            for way in range(2):
                stage2(chunk, way, d).start()

    def cross(chunk):
        for way, turn in both:
            relay(chunk, way, 1, turn).wait_recv()
            relay(chunk, way, 2, turn).wait_recv()
        for way in range(2):
            part[chunk, way, at_ring[way][0]] += got1[chunk, way, 1] + got1[chunk, way, 2]
        second(chunk)

    def cross_direct(chunk):
        for way in range(2):
            for d in (1, 3, 2):
                stage1(chunk, way, d).wait_recv()
        for way in range(2):
            part[chunk, way, at_ring[way][0]] += got1[chunk, way, 0] + (got1[chunk, way, 1] + got1[chunk, way, 2])
        second(chunk)

    def finish(h, quarter):
        chunk = h * 4 + quarter
        for way in range(2):
            for d in (1, 3, 2):
                stage2(chunk, way, d).wait_recv()
            v = ((part[chunk, way, at_ring[way][0], at_ring[1 - way][0]] + got2[chunk, way, 0])
                 + (got2[chunk, way, 1] + got2[chunk, way, 2]))
            out[:, h * 8:(h + 1) * 8, quarter * 256 + way * 128:quarter * 256 + way * 128 + 128] = v.reshape(4, 8, 128)

    def gather(h):
        for d in (1, 3, 2):
            to_z(h, d).start()

    def pass_on(h, places):
        for place in places:
            o = OFFSETS[place]
            to_z(h, 4 - o).wait_recv()
            to_pair(h, o).start()

    def arrive(h, places):
        for place in places:
            to_pair(h, OFFSETS[place]).wait_recv()
            split_lags(h, place)

    pl.semaphore_wait(barrier, len(partners))
    gather(0)
    for h in range(2):
        to_pair(h, 0).start()
    fetch(0, 0).wait()
    split_band(0, 0)
    fetch(2, 0).start()
    fetch(1, 1).wait()
    split_band(1, 1)
    fetch(3, 1).start()

    def own(h, first, count):
        def step(i, _):
            for n in range(count):
                add_products(h, first + i * count + n, 0, 1, fresh=True)
            return 0

        return step

    arrive(0, (0,))
    lax.fori_loop(0, 2, own(0, 0, 2), 0)
    pass_on(0, (1, 2))
    gather(1)
    fetch(2, 0).wait()
    split_band(2, 0)
    arrive(1, (0,))
    lax.fori_loop(0, 2, own(1, 0, 2), 0)
    pass_on(0, (3,))
    fetch(3, 1).wait()
    split_band(3, 1)
    arrive(0, (1, 2, 3))
    for quarter in range(2):
        add_products(0, quarter, 1, 4)
        begin(quarter)

    def rest(chunk, _):
        @pl.when(chunk == 3)
        def _():
            pass_on(1, (1, 2, 3))

        @pl.when(chunk == 4)
        def _():
            arrive(1, (1, 2, 3))

        add_products(chunk // 4, lax.rem(chunk, 4), 1, 4)

        @pl.when(chunk < 7)
        def _():
            begin(chunk)

        pass_sums(chunk - 2)

        @pl.when(chunk >= 4)
        def _():
            cross(chunk - 4)
        return 0

    lax.fori_loop(2, 8, rest, 0)
    begin_direct(7)
    cross(4)
    pass_sums(6)
    cross(5)
    for quarter in range(3):
        finish(0, quarter)
    cross_direct(7)
    cross(6)
    finish(0, 3)
    for quarter in range(4):
        finish(1, quarter)

    for h in range(2):
        for d in (1, 2, 3):
            to_z(h, d).wait_send()
        for o in range(4):
            to_pair(h, o).wait_send()

    def sent(chunk, _):
        for way, turn in both:
            for kind in range(3):
                relay(chunk, way, kind, turn).wait_send()
        return 0

    lax.fori_loop(0, 7, sent, 0)
    for way in range(2):
        for d in (1, 2, 3):
            stage1(7, way, d).wait_send()

    def sent_second(chunk, _):
        for way in range(2):
            for d in (1, 2, 3):
                stage2(chunk, way, d).wait_send()
        return 0

    lax.fori_loop(0, 8, sent_second, 0)


def on_device(response, focusing):
    dma = pltpu.SemaphoreType.DMA
    return pl.pallas_call(
        kernel,
        out_shape=jax.ShapeDtypeStruct((4, 16, 1024), F32),
        in_specs=[pl.BlockSpec(memory_space=pl.ANY), pl.BlockSpec(memory_space=pltpu.VMEM)],
        out_specs=pl.BlockSpec(memory_space=pltpu.VMEM),
        scratch_shapes=[
            pltpu.VMEM((2, 8, 1024, 128), F32),
            pltpu.VMEM((3, 2, 1024, 2048), BF16),
            pltpu.VMEM((2, 4, 2, 288, 128), F32),
            pltpu.VMEM((568, 128), F32),
            pltpu.VMEM((2, 3, 2, 256, 2048), BF16),
            pltpu.VMEM((8, 2, 4, 4, 32, 128), F32),
            pltpu.VMEM((8, 2, 3, 4, 32, 128), F32),
            pltpu.VMEM((8, 2, 3, 32, 128), F32),
            dma((4,)), dma((2, 3)), dma((2, 4)), dma((2, 4, 2)),
            dma((8, 2, 3, 2)), dma((8, 2, 3, 2)), dma((8, 2, 3)), dma((8, 2, 3)),
        ],
        compiler_params=pltpu.CompilerParams(
            collective_id=0, has_side_effects=True, vmem_limit_bytes=63 * 2**20),
    )(response, jnp.swapaxes(focusing, 1, 2))


def solution(mesh):
    in_specs = (P(None, "rcv", "src"), P(None, None, ("src", "rcv")))
    return jax.shard_map(
        on_device, mesh=mesh, in_specs=in_specs, out_specs=P("src", None, "rcv"), check_vma=False
    )
```
